32 devices in a mesh: fsdp: 8 (over y, x, core), seq: 4 (over z).
Axes of the slice: x: 2, y: 2, z: 4, core: 2. Of those that a mesh axis runs over, the one named last changes fastest.
Arguments:
- tokens: bfloat16 [64, 512, 768], P('fsdp', 'seq'), may hold values from -6 to 6
- lengths: int32 [64, 26], P('fsdp'), may hold values from 0 to 512, as said below
- cotangent: bfloat16 [64, 512, 768], P('fsdp', 'seq'), may hold values from -6 to 6
- project_weight: bfloat16 [768, 2304], P(('fsdp', 'seq')), may hold values from -0.21875 to 0.21875
- project_bias: bfloat16 [1536], P(('fsdp', 'seq')), may hold values from -3 to 3
- output_weight: bfloat16 [768, 768], P(('fsdp', 'seq')), may hold values from -0.875 to 0.875
- output_bias: bfloat16 [768], P(('fsdp', 'seq')), may hold values from -3 to 3
- first_gain: bfloat16 [768], P(('fsdp', 'seq')), may hold values from 0.099609375 to 1.8984375
- first_shift: bfloat16 [768], P(('fsdp', 'seq')), may hold values from -3 to 3
- expand_weight: bfloat16 [768, 3072], P(('fsdp', 'seq')), may hold values from -0.21875 to 0.21875
- expand_bias: bfloat16 [3072], P(('fsdp', 'seq')), may hold values from -3 to 3
- reduce_weight: bfloat16 [3072, 768], P(('fsdp', 'seq')), may hold values from -0.109375 to 0.109375
- reduce_bias: bfloat16 [768], P(('fsdp', 'seq')), may hold values from -3 to 3
- second_gain: bfloat16 [768], P(('fsdp', 'seq')), may hold values from 0.099609375 to 1.8984375
- second_shift: bfloat16 [768], P(('fsdp', 'seq')), may hold values from -3 to 3
Outputs:
- activations: bfloat16 [64, 512, 768], P('fsdp', 'seq')
- input_grad: float32 [64, 512, 768], P('fsdp', 'seq')
- project_grad: float32 [768, 2304], P(('fsdp', 'seq'))
- projbias_grad: float32 [1536], P(('fsdp', 'seq'))
- output_grad: float32 [768, 768], P(('fsdp', 'seq'))
- outbias_grad: float32 [768], P(('fsdp', 'seq'))
- firstgain_grad: float32 [768], P(('fsdp', 'seq'))
- firstshift_grad: float32 [768], P(('fsdp', 'seq'))
- expand_grad: float32 [768, 3072], P(('fsdp', 'seq'))
- expbias_grad: float32 [3072], P(('fsdp', 'seq'))
- reduce_grad: float32 [3072, 768], P(('fsdp', 'seq'))
- redbias_grad: float32 [768], P(('fsdp', 'seq'))
- secondgain_grad: float32 [768], P(('fsdp', 'seq'))
- secondshift_grad: float32 [768], P(('fsdp', 'seq'))
The draws below stay inside these ranges and needn't reach their ends.
Inputs may be any that keep to these rules, and one draw needn't show every extreme that they name: Row r lists the lengths of the documents packed in order into sequence r; each row sums to 512; entries after the last document are 0; a document that is not its sequence's last has 20 to 200 tokens unless it fills the whole sequence.
All inputs are finite; a program needn't handle non-finite values.
Results may differ from the reference program's by a relative error of at most 0.013.
The reference program's roundings to bfloat16 on the way count: a program that leaves them out, or rounds other values in their place, can miss the bound.
Values may be sent and summed in bfloat16 or wider, within the bound.
A program may use at most 192 MiB of HBM per device.

```python
import math
import jax
import jax.numpy as jnp
from jax import lax

D = 768
HEADS = 12
HEAD_DIM = 64
FF = 3072
SEQ_LEN = 512
DOC_MIN = 20
DOC_MAX = 200
SEQS_DEV = 8
DOCS = 26
NSEQ = 64


def draw_lengths(key, part):
    key = jax.random.fold_in(key, 11)
    first_key, second_key = jax.random.split(key)
    raw_lengths = jax.random.randint(first_key, (NSEQ, DOCS), DOC_MIN, DOC_MAX + 1)
    chosen = jax.random.randint(second_key, (NSEQ // SEQS_DEV,), 0, SEQS_DEV)
    row_ids = jnp.arange(NSEQ, dtype=jnp.int32)
    whole_row = row_ids % SEQS_DEV == chosen[row_ids // SEQS_DEV]
    raw_lengths = raw_lengths.at[:, 0].set(jnp.where(whole_row, SEQ_LEN, raw_lengths[:, 0]))
    clipped = jnp.minimum(jnp.cumsum(raw_lengths, axis=1), SEQ_LEN)
    begins = jnp.concatenate([jnp.zeros((NSEQ, 1), clipped.dtype), clipped[:, :-1]], axis=1)
    return (clipped - begins).astype(jnp.int32)


def raised(drawn, rng, source, target, shards_of, factor):
    owner, partner = [(jnp.arange(drawn.shape[position]) // (drawn.shape[position] // shards_of)).reshape([-1 if axis == position else 1 for axis in range(drawn.ndim)]) for position in (source, target)]
    chosen = jax.random.permutation(rng, shards_of)[partner]
    strong = (owner == chosen) | (owner == (partner + shards_of // 2) % shards_of)
    return jnp.where(strong, factor * drawn, drawn)


def levels(rng, shape, cuts, low, top_value):
    loudness, own = 1.0, jax.random.fold_in(rng, 6)
    for dim, parts in cuts:
        steps = jnp.exp(jax.random.uniform(jax.random.fold_in(own, dim), (parts,), jnp.float32, low / len(cuts), top_value / len(cuts)))
        loudness = loudness * jnp.repeat(steps, shape[dim] // parts).reshape([-1 if axis == dim else 1 for axis in range(len(shape))])
    return loudness


def scatter_about(stream_key, extent, scale, most, shards=(), held_as=jnp.bfloat16):
    values = scale * jax.random.normal(stream_key, extent, jnp.float32)
    if shards:
        values = values * levels(stream_key, extent, shards, -0.22, 0.18)
    return jnp.clip(values, -most, most).astype(held_as)


def heavy_noise(key, shape, scale, limit, cuts, heavy, kind=jnp.bfloat16):
    entries = scale * jax.random.normal(key, shape, jnp.float32)
    if cuts:
        entries = entries * levels(key, shape, cuts, -0.22, 0.18)
    return jnp.clip(raised(entries, jax.random.fold_in(key, 3), *heavy), -limit, limit).astype(kind)


def setup_inputs(seed: int = 0) -> dict:
    splits = jax.random.split(jax.random.key(seed), 16)
    return {
        "tokens": heavy_noise(splits[0], (NSEQ, SEQ_LEN, D), 1.0, 6.0, ((0, 8), (1, 4)), (0, 2, 8, 2.0)),
        "lengths": draw_lengths(jax.random.fold_in(splits[15], 71), 0),
        "cotangent": heavy_noise(splits[2], (NSEQ, SEQ_LEN, D), 1.0, 6.0, ((0, 8), (1, 4)), (0, 2, 8, 2.0)),
        "project_weight": scatter_about(splits[3], (D, 3 * D), D ** -0.5, 0.21875, ((0, 32),)),
        "project_bias": scatter_about(splits[4], (2 * D,), 0.5, 3.0, ((0, 32),)),
        "output_weight": scatter_about(splits[5], (D, D), (D // 16) ** -0.5, 0.875, ((0, 32),)),
        "output_bias": scatter_about(splits[6], (D,), 0.5, 3.0, ((0, 32),)),
        "first_gain": jnp.clip(1.0 + 0.18 * jax.random.normal(splits[7], (D,), jnp.float32), 0.099609375, 1.8984375).astype(jnp.bfloat16),
        "first_shift": scatter_about(splits[8], (D,), 0.5, 3.0, ((0, 32),)),
        "expand_weight": scatter_about(splits[9], (D, FF), D ** -0.5, 0.21875, ((0, 32),)),
        "expand_bias": scatter_about(splits[10], (FF,), 0.5, 3.0, ((0, 32),)),
        "reduce_weight": scatter_about(splits[11], (FF, D), FF ** -0.5, 0.109375, ((0, 32),)),
        "reduce_bias": scatter_about(splits[12], (D,), 0.5, 3.0, ((0, 32),)),
        "second_gain": jnp.clip(1.0 + 0.18 * jax.random.normal(splits[13], (D,), jnp.float32), 0.099609375, 1.8984375).astype(jnp.bfloat16),
        "second_shift": scatter_about(splits[14], (D,), 0.5, 3.0, ((0, 32),)),
    }


EPSILON = 1e-05
HIGHEST = lax.Precision.HIGHEST

@jax.custom_vjp
def low(v):
    return lax.optimization_barrier(v.astype(jnp.bfloat16)).astype(jnp.float32)

@jax.custom_vjp
def low_back(v):
    return v

def low_keep(v):
    return (low(v), None)

def low_pass(kept, grad):
    return (grad,)

def back_keep(v):
    return (v, None)

def back_low(kept, grad):
    return (low(grad),)
low.defvjp(low_keep, low_pass)
low_back.defvjp(back_keep, back_low)

def layer_norm(values, gain, shift):
    centre = values - lax.optimization_barrier(jnp.mean(values, axis=-1, keepdims=True))
    spread = lax.optimization_barrier(jnp.mean(centre * centre, axis=-1, keepdims=True))
    return centre * lax.rsqrt(spread + EPSILON) * gain + shift

def gelu_exact(values):
    return jax.nn.gelu(values, approximate=False)

def matmul(left, right):
    return jnp.dot(left, right, precision=HIGHEST, preferred_element_type=jnp.float32)

def encoder(inputs, allowed, params):
    proj, pbias, outw, obias, gain_one, shift_one, expand, ebias, reduce_w, rbias, gain_two, shift_two = params
    batch = inputs.shape[0]
    flattened = inputs.reshape(-1, D)
    full_bias = jnp.concatenate([pbias[:D], jnp.zeros((D,), jnp.float32), pbias[D:]])
    projected = low_back(low(matmul(flattened, proj) + full_bias))
    queries = projected[:, :D].reshape(batch, SEQ_LEN, HEADS, HEAD_DIM)
    keys = projected[:, D:2 * D].reshape(batch, SEQ_LEN, HEADS, HEAD_DIM)
    values = projected[:, 2 * D:].reshape(batch, SEQ_LEN, HEADS, HEAD_DIM)
    scores = low_back(jnp.einsum('bqhd,bkhd->bhqk', queries, keys, precision=HIGHEST) * HEAD_DIM ** (-0.5))
    scores = jnp.where(allowed[:, None], scores, -1e+30)
    probabilities = low(jax.nn.softmax(scores, axis=-1))
    mixed = low_back(low(jnp.einsum('bhqk,bkhd->bqhd', probabilities, values, precision=HIGHEST))).reshape(-1, D)
    attention = low_back(matmul(mixed, outw) + obias)
    first = layer_norm(flattened + attention, gain_one, shift_one)
    inner_pre = low_back(matmul(low(first), expand) + ebias)
    hidden = low(gelu_exact(inner_pre))
    branch_out = low_back(matmul(hidden, reduce_w) + rbias)
    return layer_norm(first + branch_out, gain_two, shift_two).reshape(batch, SEQ_LEN, D)

def reference(tokens, lengths, cotangent, project_weight, project_bias, output_weight, output_bias, first_gain, first_shift, expand_weight, expand_bias, reduce_weight, reduce_bias, second_gain, second_shift):
    params = tuple((weight.astype(jnp.float32) for weight in (project_weight, project_bias, output_weight, output_bias, first_gain, first_shift, expand_weight, expand_bias, reduce_weight, reduce_bias, second_gain, second_shift)))
    nseq_all = tokens.shape[0]
    per_group = math.gcd(nseq_all, 8)
    positions = jnp.arange(SEQ_LEN, dtype=jnp.int32)
    doc_ends = jnp.cumsum(lengths, axis=1)
    segments = lax.optimization_barrier(jnp.sum((positions[None, :, None] >= doc_ends[:, None, :]).astype(jnp.int32), axis=2))

    def grouped(array):
        return array.reshape((nseq_all // per_group, per_group) + array.shape[1:])

    def advance(totals, pieces):
        inputs, seg_ids, grads_out = pieces
        allowed = seg_ids[:, :, None] == seg_ids[:, None, :]
        result, pullback = jax.vjp(lambda values_in, params_in: encoder(values_in, allowed, params_in), inputs.astype(jnp.float32), params)
        grad_inputs, grad_params = pullback(grads_out.astype(jnp.float32))
        totals = tuple((total_now + grad_now for total_now, grad_now in zip(totals, grad_params)))
        return (totals, (result.astype(jnp.bfloat16), grad_inputs))
    initial = tuple((jnp.zeros(param.shape, jnp.float32) for param in params))
    totals, (outputs, grads_in) = lax.scan(advance, initial, (grouped(tokens), grouped(segments), grouped(cotangent)))
    return (outputs.reshape(tokens.shape), grads_in.reshape(tokens.shape), totals[0], totals[1], totals[2], totals[3], totals[4], totals[5], totals[6], totals[7], totals[8], totals[9], totals[10], totals[11])
```

```python
import functools

import jax
import jax.numpy as jnp
from jax import lax
from jax.experimental import pallas as pl
from jax.experimental.pallas import tpu as pltpu
from jax.sharding import PartitionSpec as P

HEAD_DIM = 64
PAIR = 2 * HEAD_DIM
PAD = 128
VMEM_BYTES = 40 * 1024 * 1024


EPSILON = 1e-05


def layer_norm(values, gain, shift):
    centre = values - jnp.mean(values, axis=-1, keepdims=True)
    spread = jnp.mean(centre * centre, axis=-1, keepdims=True)
    return centre * lax.rsqrt(spread + EPSILON) * gain + shift


def normal_cdf(values):
    return 0.5 + 0.5 * lax.erf(values * 0.5**0.5)


def gelu_slope(values):
    density = jnp.exp(values * values * -0.5) * 0.3989422804014327
    return normal_cdf(values) + values * density


def product(left, right, contract):
    return lax.dot_general(
        left, right, (((contract[0],), (contract[1],)), ((), ())), preferred_element_type=jnp.float32
    )


def probabilities_of(query, key, allowed):
    scores = jnp.where(allowed, product(key, query, (1, 1)) * HEAD_DIM ** (-0.5), -1e30)
    exponent = jnp.exp(scores - jnp.max(scores, axis=0, keepdims=True))
    return exponent * (1.0 / jnp.sum(exponent, axis=0, keepdims=True))


def attend_kernel(query_ref, key_ref, value_ref, column_ref, row_ref, mixed_ref):
    allowed = column_ref[0] == row_ref[0]
    parts = []
    for head in range(2):
        cols = slice(head * HEAD_DIM, (head + 1) * HEAD_DIM)
        probs = probabilities_of(query_ref[:, cols], key_ref[:, cols], allowed)
        mixed = product(value_ref[:, cols], probs.astype(jnp.bfloat16), (0, 0))
        parts.append(mixed.T)
    mixed_ref[...] = jnp.concatenate(parts, axis=1).astype(jnp.bfloat16)


def attend_back_kernel(
    query_ref, key_ref, value_ref, grad_ref, column_ref, row_ref, out_ref
):
    allowed = column_ref[0] == row_ref[0]
    scale = HEAD_DIM ** (-0.5)
    parts = []
    for head in range(2):
        cols = slice(head * HEAD_DIM, (head + 1) * HEAD_DIM)
        query, key, value = query_ref[:, cols], key_ref[:, cols], value_ref[:, cols]
        grad = grad_ref[:, cols]
        probs = probabilities_of(query, key, allowed)
        grad_value = product(probs.astype(jnp.bfloat16), grad, (1, 0))
        grad_probs = product(value, grad, (1, 1))
        centred = jnp.sum(probs * grad_probs, axis=0, keepdims=True)
        grad_scores = (probs * (grad_probs - centred)).astype(jnp.bfloat16)
        grad_key = product(grad_scores, query, (1, 0)) * scale
        grad_query = (product(key, grad_scores, (0, 0)) * scale).T
        parts.append((grad_query, grad_key, grad_value))
    for place in range(3):
        out_ref[place] = jnp.concatenate(
            [parts[0][place], parts[1][place]], axis=1
        ).astype(jnp.bfloat16)


def attention_specs(length, pairs):
    column = pl.BlockSpec((1, length, 1), lambda s, h: (s, 0, 0))
    row = pl.BlockSpec((1, 1, length), lambda s, h: (s, 0, 0))
    blocks = [
        pl.BlockSpec((length, PAIR), functools.partial(lambda first, s, h: (s, first + h), k * pairs))
        for k in range(3)
    ]
    return blocks, column, row


def attend(projected, segments):
    seqs, length = segments.shape
    width = projected.shape[1] // 3
    pairs = width // PAIR
    blocks, column, row = attention_specs(length, pairs)
    cells = seqs * (width // HEAD_DIM) * length * length
    return pl.pallas_call(
        attend_kernel,
        grid=(seqs, pairs),
        out_shape=jax.ShapeDtypeStruct((seqs * length, width), jnp.bfloat16),
        in_specs=[*blocks, column, row],
        out_specs=pl.BlockSpec((length, PAIR), lambda s, h: (s, h)),
        compiler_params=pltpu.CompilerParams(vmem_limit_bytes=VMEM_BYTES),
        cost_estimate=pl.CostEstimate(
            flops=cells * 4 * HEAD_DIM, bytes_accessed=8 * seqs * length * width, transcendentals=cells
        ),
    )(projected, projected, projected, segments[:, :, None], segments[:, None, :])


def attend_back(projected, grad_mixed, segments):
    seqs, length = segments.shape
    width = projected.shape[1] // 3
    pairs = width // PAIR
    blocks, column, row = attention_specs(length, pairs)
    cells = seqs * (width // HEAD_DIM) * length * length
    return pl.pallas_call(
        attend_back_kernel,
        grid=(seqs, pairs),
        out_shape=jax.ShapeDtypeStruct((3, seqs * length, width), jnp.bfloat16),
        in_specs=[*blocks, blocks[0], column, row],
        out_specs=pl.BlockSpec((3, length, PAIR), lambda s, h: (0, s, h)),
        compiler_params=pltpu.CompilerParams(vmem_limit_bytes=VMEM_BYTES),
        cost_estimate=pl.CostEstimate(
            flops=cells * 10 * HEAD_DIM, bytes_accessed=14 * seqs * length * width, transcendentals=cells
        ),
    )(projected, projected, projected, grad_mixed, segments[:, :, None], segments[:, None, :])


def to_sequences(array):
    n, me = lax.axis_size("seq"), lax.axis_index("seq")
    some, rows, width = array.shape[0] // n, array.shape[1], array.shape[2]
    own = lax.dynamic_slice_in_dim(array, me * some, some, 0)
    whole = jnp.zeros((some, n * rows, width), array.dtype)
    whole = lax.dynamic_update_slice_in_dim(whole, own, me * rows, 1)
    for step in range(1, n):
        there, source = lax.rem(me + step, n), lax.rem(me + n - step, n)
        sent = lax.dynamic_slice_in_dim(array, there * some, some, 0)
        came = lax.ppermute(sent, "seq", [(i, (i + step) % n) for i in range(n)])
        whole = lax.dynamic_update_slice_in_dim(whole, came, source * rows, 1)
    return whole


def to_positions(array):
    n, me = lax.axis_size("seq"), lax.axis_index("seq")
    some, rows, width = array.shape[0], array.shape[1] // n, array.shape[2]
    own = lax.dynamic_slice_in_dim(array, me * rows, rows, 1)
    whole = jnp.zeros((n * some, rows, width), array.dtype)
    whole = lax.dynamic_update_slice_in_dim(whole, own, me * some, 0)
    for step in range(1, n):
        there, source = lax.rem(me + step, n), lax.rem(me + n - step, n)
        sent = lax.dynamic_slice_in_dim(array, there * rows, rows, 1)
        came = lax.ppermute(sent, "seq", [(i, (i + step) % n) for i in range(n)])
        whole = lax.dynamic_update_slice_in_dim(whole, came, source * some, 0)
    return whole


def packed_columns(vectors, rows):
    columns = jnp.concatenate([v.reshape(rows, -1) for v in vectors], axis=1)
    return jnp.pad(columns, ((0, 0), (0, PAD - columns.shape[1])))


def unpacked_columns(columns, sizes):
    rows, start, vectors = columns.shape[0], 0, []
    for size in sizes:
        wide = size // rows
        vectors.append(columns[:, start : start + wide].reshape(size))
        start += wide
    return vectors


def gathered(weight):
    return lax.all_gather(weight, ("fsdp", "seq"), axis=0, tiled=True)


def scattered(grad):
    return lax.psum_scatter(grad, ("fsdp", "seq"), scatter_dimension=0, tiled=True)


def shards(
    tokens,
    lengths,
    cotangent,
    project_weight,
    project_bias,
    output_weight,
    output_bias,
    first_gain,
    first_shift,
    expand_weight,
    expand_bias,
    reduce_weight,
    reduce_bias,
    second_gain,
    second_shift,
):
    model_width = tokens.shape[2]
    rows_own = project_weight.shape[0]
    devices = model_width // rows_own
    own_vectors = (
        project_bias, output_bias, first_gain, first_shift,
        expand_bias, reduce_bias, second_gain, second_shift,
    )
    sizes = [v.shape[0] * devices for v in own_vectors]
    first_pack = gathered(
        jnp.concatenate([project_weight, packed_columns(own_vectors, rows_own)], axis=1)
    )
    out_full = gathered(output_weight)
    expand_full = gathered(expand_weight)
    reduce_full = gathered(reduce_weight)
    inputs = to_sequences(tokens)
    grads_out = to_sequences(cotangent)
    proj_full = first_pack[:, : 3 * model_width]
    pbias, obias, gain_one, shift_one, ebias, rbias, gain_two, shift_two = (
        v.astype(jnp.float32) for v in unpacked_columns(first_pack[:, 3 * model_width :], sizes)
    )
    seqs_here, length, _ = inputs.shape
    own_lengths = lax.dynamic_slice_in_dim(
        lengths, lax.axis_index("seq") * seqs_here, seqs_here, 0
    )
    positions = jnp.arange(length, dtype=jnp.int32)
    doc_ends = jnp.cumsum(own_lengths, axis=1)
    segments = jnp.sum(
        (positions[None, :, None] >= doc_ends[:, None, :]).astype(jnp.int32), axis=2
    )
    flattened = inputs.reshape(-1, model_width)
    full_bias = jnp.concatenate(
        [pbias[:model_width], jnp.zeros((model_width,), jnp.float32), pbias[model_width:]]
    )
    projected = (
        jnp.dot(flattened, proj_full, preferred_element_type=jnp.float32) + full_bias
    ).astype(jnp.bfloat16)
    mixed_flat = attend(projected, segments)
    attention = jnp.dot(mixed_flat, out_full, preferred_element_type=jnp.float32) + obias
    residual_one = flattened.astype(jnp.float32) + attention
    first_norm = layer_norm(residual_one, gain_one, shift_one)
    first_low = first_norm.astype(jnp.bfloat16)
    inner_pre = jnp.dot(first_low, expand_full, preferred_element_type=jnp.float32) + ebias
    hidden = (inner_pre * normal_cdf(inner_pre)).astype(jnp.bfloat16)
    branch_out = jnp.dot(hidden, reduce_full, preferred_element_type=jnp.float32) + rbias
    residual_two = first_norm + branch_out
    result = layer_norm(residual_two, gain_two, shift_two).astype(jnp.bfloat16)
    activations = to_positions(result.reshape(inputs.shape))

    grad_result = grads_out.reshape(-1, model_width).astype(jnp.float32)
    norm_two_pull = jax.vjp(layer_norm, residual_two, gain_two, shift_two)[1]
    grad_residual_two, grad_gain_two, grad_shift_two = norm_two_pull(grad_result)
    grad_branch = grad_residual_two.astype(jnp.bfloat16)
    grad_reduce = product(hidden, grad_branch, (0, 0)).astype(jnp.bfloat16)
    grad_reduce, grad_branch = lax.optimization_barrier((grad_reduce, grad_branch))
    reduce_grad = scattered(grad_reduce).astype(jnp.float32)
    grad_rbias = jnp.sum(grad_branch.astype(jnp.float32), axis=0)
    grad_hidden = product(grad_branch, reduce_full, (1, 1))
    grad_inner = (gelu_slope(inner_pre) * grad_hidden).astype(jnp.bfloat16)
    grad_ebias = jnp.sum(grad_inner.astype(jnp.float32), axis=0)
    grad_expand = product(first_low, grad_inner, (0, 0)).astype(jnp.bfloat16)
    grad_expand, grad_inner = lax.optimization_barrier((grad_expand, grad_inner))
    expand_grad = scattered(grad_expand).astype(jnp.float32)
    grad_first = grad_residual_two + product(grad_inner, expand_full, (1, 1))
    norm_one_pull = jax.vjp(layer_norm, residual_one, gain_one, shift_one)[1]
    grad_residual_one, grad_gain_one, grad_shift_one = norm_one_pull(grad_first)
    grad_attention = grad_residual_one.astype(jnp.bfloat16)
    grad_outw = product(mixed_flat, grad_attention, (0, 0))
    grad_obias = jnp.sum(grad_attention.astype(jnp.float32), axis=0)
    early_vectors = (
        grad_obias, grad_gain_one, grad_shift_one,
        grad_ebias, grad_rbias, grad_gain_two, grad_shift_two,
    )
    grad_mixed = product(grad_attention, out_full, (1, 1)).astype(jnp.bfloat16)
    back = attend_back(projected, grad_mixed, segments)
    grad_projected = jnp.concatenate([back[0], back[1], back[2]], axis=1)
    grad_project = product(flattened, grad_projected, (0, 0))
    grad_column_sums = jnp.sum(grad_projected.astype(jnp.float32), axis=0)
    grad_pbias = jnp.concatenate(
        [grad_column_sums[:model_width], grad_column_sums[2 * model_width :]]
    )
    late = jnp.concatenate(
        [grad_project, grad_outw, packed_columns((grad_pbias, *early_vectors), model_width)],
        axis=1,
    ).astype(jnp.bfloat16)
    late, grad_projected = lax.optimization_barrier((late, grad_projected))
    late_pack = scattered(late).astype(jnp.float32)
    project_grad = late_pack[:, : 3 * model_width]
    output_grad = late_pack[:, 3 * model_width : 4 * model_width]
    (
        projbias_grad,
        outbias_grad,
        firstgain_grad,
        firstshift_grad,
        expbias_grad,
        redbias_grad,
        secondgain_grad,
        secondshift_grad,
    ) = unpacked_columns(late_pack[:, 4 * model_width :], [v.shape[0] for v in own_vectors])
    grad_inputs = grad_residual_one + product(grad_projected, proj_full, (1, 1))
    input_grad = to_positions(
        grad_inputs.astype(jnp.bfloat16).reshape(inputs.shape)
    ).astype(jnp.float32)
    return (
        activations,
        input_grad,
        project_grad,
        projbias_grad,
        output_grad,
        outbias_grad,
        firstgain_grad,
        firstshift_grad,
        expand_grad,
        expbias_grad,
        reduce_grad,
        redbias_grad,
        secondgain_grad,
        secondshift_grad,
    )


def solution(mesh):
    in_specs = (
        P("fsdp", "seq", None),
        P("fsdp", None),
        P("fsdp", "seq", None),
        P(("fsdp", "seq"), None),
        P(("fsdp", "seq")),
        P(("fsdp", "seq"), None),
        P(("fsdp", "seq")),
        P(("fsdp", "seq")),
        P(("fsdp", "seq")),
        P(("fsdp", "seq"), None),
        P(("fsdp", "seq")),
        P(("fsdp", "seq"), None),
        P(("fsdp", "seq")),
        P(("fsdp", "seq")),
        P(("fsdp", "seq")),
    )
    out_specs = (
        P("fsdp", "seq", None),
        P("fsdp", "seq", None),
        P(("fsdp", "seq"), None),
        P(("fsdp", "seq")),
        P(("fsdp", "seq"), None),
        P(("fsdp", "seq")),
        P(("fsdp", "seq")),
        P(("fsdp", "seq")),
        P(("fsdp", "seq"), None),
        P(("fsdp", "seq")),
        P(("fsdp", "seq"), None),
        P(("fsdp", "seq")),
        P(("fsdp", "seq")),
        P(("fsdp", "seq")),
    )
    return jax.shard_map(shards, mesh=mesh, in_specs=in_specs, out_specs=out_specs, check_vma=False)
```
